512 devices in a mesh: row: 32 (over y, x), col: 16 (over z, core).
Axes of the slice: x: 4, y: 8, z: 8, core: 2. Of those that a mesh axis runs over, the one named last changes fastest.
Arguments:
- a_vals: bfloat16 [32, 256, 64, 2048], P('row', 'col'), may hold values from -0.25 to 0.25
- a_cols: int32 [32, 256, 32], P('row', 'col'), may hold values from 0 to 767, as said below
- a_count: int32 [32, 256], P('row', 'col'), may hold values from 4 to 32, as said below
- p_vals: bfloat16 [32, 256, 64, 128], P('row', 'col'), may hold values from -6 to 6
- p_cols: int32 [32, 256, 2], P('row', 'col'), may hold values from 0 to 15, as said below
- r_vals: bfloat16 [32, 256, 64, 128], P('row', 'col'), may hold values from -0.125 to 0.125
- r_cols: int32 [32, 256, 2], P('row', 'col'), may hold values from 0 to 15, as said below
Outputs:
- coarse: float32 [32, 1024, 960], P('row', 'col')
The draws below stay inside these ranges and needn't reach their ends.
Inputs may be any that keep to these rules, and one draw needn't show every extreme that they name: `a_cols`: the entries of a row are distinct. Every entry is s * 256 + t with t = (q + o) mod 256 for the row's block q and some o with -8 <= o <= 8; q itself appears with s = 0, 1 and 2, and every row has an entry with o = 8 or o = -8. `a_count`: in each plane, the 31 blocks nearest one block (around the plane) have 32 live slots; the other rows have from 4 to min(10, 32). `p_cols`: A row of block q holds, in either order, the aggregate q // 16 and the aggregate beside it on the side of q's half of its aggregate: (q // 16 - 1) mod 16 where q % 16 < 8, else (q // 16 + 1) mod 16. `r_cols`: A row of block q holds the same two aggregates as p_cols[z, q], in an order of its own.
All inputs are finite; a program needn't handle non-finite values.
Results may differ from the reference program's by a relative error of at most 0.0029.
Values may be sent and summed in bfloat16 or wider, within the bound.
No kernel may reach another device: no remote copies, remote signals or barrier semaphores. Data moves between devices by JAX's collectives and lax.ppermute only.
A program may use at most 128 MiB of HBM per device.

```python
import jax
import jax.numpy as jnp
from jax import lax

B = 64
PLANE = 256
AGG = 16
WIN = 8
KA = 32
KP = 2
KR = 2
NCP = 16
NZ = 32


def row_permutations(key, row_total, length):
    keys = jax.random.split(key, row_total)
    return jax.vmap(lambda single: jax.random.permutation(single, length))(keys).astype(jnp.int32)


def draw_a_cols(key, part):
    row_total = NZ * PLANE
    owned_block_index = jnp.tile(jnp.arange(PLANE, dtype=jnp.int32), NZ)
    reach_span = 2 * WIN
    forced_pick = jax.random.randint(jax.random.fold_in(key, 100), (row_total,), 0, 6)
    forced = forced_pick // 2 * reach_span + forced_pick % 2 * (reach_span - 1)
    remaining = row_permutations(jax.random.fold_in(key, 101), row_total, 3 * reach_span - 1)[:, :KA - 4]
    remaining = remaining + (remaining >= forced[:, None]).astype(jnp.int32)
    chosen = jnp.concatenate([forced[:, None], remaining], axis=1)
    band_of = chosen // reach_span
    place_in = chosen % reach_span
    offset = place_in - WIN + (place_in >= WIN).astype(jnp.int32)
    linked = band_of * PLANE + (owned_block_index[:, None] + offset) % PLANE
    entries = jnp.concatenate([(PLANE + owned_block_index)[:, None], owned_block_index[:, None], (2 * PLANE + owned_block_index)[:, None], linked], axis=1)
    slot_order = row_permutations(jax.random.fold_in(key, 102), row_total, KA)
    shuffled = jnp.take_along_axis(entries, slot_order, axis=1)
    return shuffled.reshape(NZ, PLANE, KA).astype(jnp.int32)


def draw_a_count(key, part):
    blocks = jnp.arange(PLANE, dtype=jnp.int32)[None, :]
    centre = jax.random.randint(jax.random.fold_in(key, 201), (NZ, 1), 0, PLANE)
    distance = jnp.abs(blocks - centre)
    circular = jnp.minimum(distance, PLANE - distance)
    light_count = jax.random.randint(jax.random.fold_in(key, 202), (NZ, PLANE), 4, min(10, KA) + 1)
    return jnp.where(circular < AGG, KA, light_count).astype(jnp.int32)


def coarse_slots(key, salt):
    blocks = jnp.arange(PLANE, dtype=jnp.int32)
    own_agg = blocks // AGG
    near_agg = jnp.where(blocks % AGG < AGG // 2, (own_agg - 1) % NCP, (own_agg + 1) % NCP)
    flipped = jax.random.randint(jax.random.fold_in(key, salt), (NZ, PLANE), 0, 2)
    first_slot = jnp.where(flipped == 0, own_agg[None, :], near_agg[None, :])
    second_slot = jnp.where(flipped == 0, near_agg[None, :], own_agg[None, :])
    return jnp.stack([first_slot, second_slot], axis=2).astype(jnp.int32)


def draw_p_cols(key, part):
    return coarse_slots(key, 401)


def draw_r_cols(key, part):
    return coarse_slots(key, 402)


def levels(key, extent, cuts, low, high):
    gain = 1.0
    for dim, shards_of in cuts:
        heights = jax.random.uniform(jax.random.fold_in(jax.random.fold_in(key, 6), dim), (shards_of,), jnp.float32, low / len(cuts), high / len(cuts))
        gain = gain * jnp.repeat(jnp.exp(heights), extent[dim] // shards_of).reshape((-1,) + (1,) * (len(extent) - 1 - dim))
    return gain


def scatter_about(rng, dims, deviation, reach, shards=(), held_as=jnp.bfloat16):
    values = jax.random.normal(rng, dims, jnp.float32) * deviation
    if len(shards) > 0:
        values = levels(rng, dims, shards, -0.22, 0.18) * values
    return jnp.clip(values, min=-reach, max=reach).astype(held_as)


def setup_inputs(seed: int = 0) -> dict:
    seeds = jax.random.split(jax.random.key(seed), 8)
    a_vals = scatter_about(seeds[0], (NZ, PLANE, B, KA * B), (8 * B) ** -0.5, 0.25, ((0, 32), (1, 16)))
    a_cols = draw_a_cols(jax.random.fold_in(seeds[7], 71), 0)
    a_count = draw_a_count(jax.random.fold_in(seeds[7], 71), 0)
    p_vals = scatter_about(seeds[3], (NZ, PLANE, B, KP * B), 1.0, 6.0, ((0, 32), (1, 16)))
    p_cols = draw_p_cols(jax.random.fold_in(seeds[7], 71), 0)
    r_vals = scatter_about(seeds[5], (NZ, PLANE, B, KR * B), (2 * AGG * B) ** -0.5, 0.125, ((0, 32), (1, 16)))
    r_cols = draw_r_cols(jax.random.fold_in(seeds[7], 71), 0)
    return {"a_vals": a_vals, "a_cols": a_cols, "a_count": a_count, "p_vals": p_vals, "p_cols": p_cols, "r_vals": r_vals, "r_cols": r_cols}


def fine_block_row(plane_index, block_index, a_vals, a_cols, a_count, p_vals, p_cols):
    link_ids = a_cols[plane_index, block_index]
    band_of = link_ids // PLANE
    target = link_ids % PLANE
    source_plane = plane_index + band_of - 1
    inside = (source_plane >= 0) & (source_plane < NZ)
    clipped = jnp.clip(source_plane, 0, NZ - 1).astype(jnp.int32)
    live_slot = (jnp.arange(KA, dtype=jnp.int32) < a_count[plane_index, block_index]) & inside
    selected_values = p_vals[clipped, target].astype(jnp.float32).reshape(KA, B, KP, B)
    picked_cols = p_cols[clipped, target]
    target_aggregate = target // AGG
    own_agg = block_index // AGG
    slot_window = (picked_cols - target_aggregate[:, None] + 1) % NCP
    agg_shift = (target_aggregate - own_agg + 1) % NCP - 1
    frame_of = slot_window + agg_shift[:, None]
    three = jnp.arange(3, dtype=jnp.int32)
    band_hit = band_of[:, None, None] == three[None, None, :]
    frame_hit = frame_of[:, :, None] == three[None, None, :]
    placing = (band_hit[:, :, :, None] & frame_hit[:, :, None, :] & live_slot[:, None, None, None]).astype(jnp.float32)
    coupling_weight = a_vals[plane_index, block_index].astype(jnp.float32).reshape(B, KA, B)
    triple_product = jnp.einsum("ltg,tgfy->tfly", coupling_weight, selected_values, precision=lax.Precision.HIGHEST)
    return jnp.einsum("kmbc,kmsi->bsic", triple_product, placing, precision=lax.Precision.HIGHEST)


def coarse_plane(plane_index, a_vals, a_cols, a_count, p_vals, p_cols, r_vals, r_cols):
    def one_block(block_index):
        return fine_block_row(plane_index, block_index, a_vals, a_cols, a_count, p_vals, p_cols)

    row_terms = jax.vmap(one_block)(jnp.arange(PLANE, dtype=jnp.int32))
    rounded = lax.optimization_barrier(row_terms.astype(jnp.bfloat16))
    fine_rows = rounded.astype(jnp.float32)
    restrict = r_vals[plane_index].astype(jnp.float32).reshape(PLANE, B, KR, B)
    blocks = jnp.arange(PLANE, dtype=jnp.int32)
    own_agg = blocks // AGG
    row_cols = r_cols[plane_index]
    offset = (row_cols - own_agg[:, None] + 1) % NCP - 1
    partial_value = jnp.einsum("qbld,qbsie->qldsie", restrict, fine_rows, precision=lax.Precision.HIGHEST)
    row_hit = row_cols[:, :, None] == jnp.arange(NCP, dtype=jnp.int32)[None, None, :]
    five = jnp.arange(5, dtype=jnp.int32)
    three = jnp.arange(3, dtype=jnp.int32)
    col_hit = five[None, None, :, None] == three[None, None, None, :] - offset[:, :, None, None] + 1
    placing = (row_hit[:, :, :, None, None] & col_hit[:, :, None, :, :]).astype(jnp.float32)
    coarse = jnp.einsum("qldsie,qlcri->cdsre", partial_value, placing, precision=lax.Precision.HIGHEST)
    return coarse.reshape(NCP * B, 15 * B)


def reference(a_vals, a_cols, a_count, p_vals, p_cols, r_vals, r_cols):
    def one_plane(plane_index):
        return coarse_plane(plane_index, a_vals, a_cols, a_count, p_vals, p_cols, r_vals, r_cols)

    return lax.map(one_plane, jnp.arange(NZ, dtype=jnp.int32))
```

```python
import jax
import jax.numpy as jnp
from jax import lax
from jax.experimental import pallas as pl
from jax.experimental.pallas import tpu as pltpu
from jax.sharding import PartitionSpec as P

PLANE = 256
AGG = 16
HALF = 8
B = 64
KA = 32
PAIR = 2 * B
TILES = KA // 2
EMPTY = 2 * TILES
SPAN = 24
DEPTH = HALF * B

F32 = jnp.float32
BF16 = jnp.bfloat16


def shift_cols(value, step):
    count = lax.axis_size("col")
    return lax.ppermute(value, "col", [(i, (i + step) % count) for i in range(count)])


def swap_rows(value, first):
    pairs = []
    for row in range(first, lax.axis_size("row") - 1, 2):
        pairs += [(row, row + 1), (row + 1, row)]
    return lax.ppermute(value, "row", pairs)


def plane_of(first):
    return 2 * lax.rem(lax.axis_index("row") + first + 1, 2)


def swap_lanes(x):
    return pltpu.roll(x, B, 1)


def flip_mask(cols_ref, q):
    first_own = cols_ref[0:1, q : q + 1] == lax.axis_index("col")
    value = jnp.where(first_own, 1.0, 0.0) if q < HALF else jnp.where(first_own, 0.0, 1.0)
    return jnp.broadcast_to(value, (B, PAIR)) > 0.5


def ordered(x, cols_ref, q):
    return jnp.where(flip_mask(cols_ref, q), swap_lanes(x), x)


def order_kernel(cols_hbm, p_hbm, all_ref, head_ref, tail_ref, cols_ref, raw, sems):
    parts = 4
    size = AGG // parts
    cols_copy = pltpu.make_async_copy(cols_hbm, cols_ref, sems.at[parts])
    cols_copy.start()

    def fetch(part):
        at = pl.ds(part * size, size)
        return pltpu.make_async_copy(p_hbm.at[0, at], raw.at[at], sems.at[part])

    for part in range(parts):
        fetch(part).start()
    cols_copy.wait()
    for part in range(parts):
        fetch(part).wait()
        for q in range(part * size, (part + 1) * size):
            y = ordered(raw[q], cols_ref, q)
            all_ref[q] = y
            if q < HALF:
                head_ref[q] = y
            else:
                tail_ref[q - HALF] = y


def order(p_vals, p_cols):
    half = jax.ShapeDtypeStruct((HALF, B, PAIR), BF16)
    return pl.pallas_call(
        order_kernel,
        out_shape=(jax.ShapeDtypeStruct((AGG, B, PAIR), BF16), half, half),
        in_specs=[pl.BlockSpec(memory_space=pl.ANY)] * 2,
        out_specs=tuple(whole(3)),
        scratch_shapes=[
            pltpu.VMEM((2, AGG), jnp.int32),
            pltpu.VMEM((AGG, B, PAIR), BF16),
            pltpu.SemaphoreType.DMA((5,)),
        ],
        compiler_params=pltpu.CompilerParams(vmem_limit_bytes=4 << 20),
        name="order",
    )(in_hbm(p_cols[0].T), in_hbm(p_vals))


def prepare_kernel(cols_hbm, a_hbm, r_hbm, slots_ref, restrict_ref, cols_ref, raw, sems, r_sem, cols_sem):
    def fetch(q):
        return pltpu.make_async_copy(a_hbm.at[0, q], slots_ref.at[q, :, pl.ds(0, KA * B)], sems.at[q])

    for q in range(AGG):
        fetch(q).start()
    r_copy = pltpu.make_async_copy(r_hbm.at[0], raw, r_sem)
    r_copy.start()
    cols_copy = pltpu.make_async_copy(cols_hbm, cols_ref, cols_sem)
    cols_copy.start()

    def row(q, carry):
        slots_ref[q, :, EMPTY * PAIR :] = jnp.zeros((B, PAIR), BF16)
        fetch(q).wait()
        for k in range(TILES):
            x = slots_ref[q, :, k * PAIR : (k + 1) * PAIR]
            slots_ref[q, :, (TILES + k) * PAIR : (TILES + k + 1) * PAIR] = swap_lanes(x)
        return carry

    lax.fori_loop(0, AGG, row, 0)
    r_copy.wait()
    cols_copy.wait()
    for q in range(0, AGG, 2):
        two = jnp.concatenate([ordered(raw[q], cols_ref, q), ordered(raw[q + 1], cols_ref, q + 1)], axis=0)
        at = (q % HALF) * B
        restrict_ref[q // HALF, :, at : at + PAIR] = two.T


def prepare(r_cols, a_vals, r_vals):
    return pl.pallas_call(
        prepare_kernel,
        out_shape=(
            pltpu.VMEM((AGG, B, (EMPTY + 1) * PAIR), BF16),
            jax.ShapeDtypeStruct((2, PAIR, DEPTH), BF16),
        ),
        in_specs=[pl.BlockSpec(memory_space=pl.ANY)] * 3,
        out_specs=tuple(whole(2)),
        scratch_shapes=[
            pltpu.VMEM((2, AGG), jnp.int32),
            pltpu.VMEM((AGG, B, PAIR), BF16),
            pltpu.SemaphoreType.DMA((AGG,)),
            pltpu.SemaphoreType.DMA,
            pltpu.SemaphoreType.DMA,
        ],
        compiler_params=pltpu.CompilerParams(vmem_limit_bytes=12 << 20),
        cost_estimate=pl.CostEstimate(flops=0, bytes_accessed=6 << 20, transcendentals=0),
        name="prepare",
    )(
        in_hbm(r_cols[0].T),
        in_hbm(a_vals),
        in_hbm(r_vals),
    )


def placed(x, shifted):
    if not shifted:
        return x
    lower = lax.broadcasted_iota(jnp.int32, (B, PAIR), 1) < B
    first, second = swap_lanes(x[:, :PAIR]), swap_lanes(x[:, PAIR:])
    return jnp.concatenate([jnp.where(lower, 0.0, first), jnp.where(lower, first, second)], axis=1)


def merged(low, high):
    lower = lax.broadcasted_iota(jnp.int32, (DEPTH, PAIR), 1) < B
    high = swap_lanes(high)
    return low + jnp.where(lower, 0.0, high), jnp.where(lower, high, 0.0)


def rows_of(ref, start):
    return ref[start : start + HALF].reshape(DEPTH, PAIR)


def gather(index_ref, slots_ref, s, half, j, into):
    lower = lax.broadcasted_iota(jnp.int32, (B, PAIR), 1) < B
    for e in range(HALF):
        q = half * HALF + e
        at = q * (3 * SPAN) + s * SPAN + j * HALF
        for tile in range(HALF // 2):
            rows, cols = slice(e * B, (e + 1) * B), slice(tile * PAIR, (tile + 1) * PAIR)
            if (j == 0 and tile < e // 2) or (j == 2 and tile > e // 2):
                into[rows, cols] = jnp.zeros((B, PAIR), BF16)
                continue
            first = pl.multiple_of(index_ref[at + 2 * tile] * PAIR, PAIR)
            second = pl.multiple_of(index_ref[at + 2 * tile + 1] * PAIR, PAIR)
            into[rows, cols] = jnp.where(
                lower, slots_ref[q, :, pl.ds(first, PAIR)], slots_ref[q, :, pl.ds(second, PAIR)]
            )


def middle_kernel(
    index_ref, slots_ref, restrict_ref, left_ref, own_ref, right_ref, own_out, before_out, after_out, band
):
    parts = [(left_ref, 0), (own_ref, 0), (own_ref, HALF), (right_ref, 0)]
    terms = []
    turn = 0
    for half in range(2):
        sums = [None, None]
        for j in range(3):
            turn = (turn + 1) % 3
            gather(index_ref, slots_ref, 1, half, j, band.at[turn])
            term = jnp.dot(band[turn], rows_of(*parts[half + j]), preferred_element_type=F32)
            side = (half + j) // 2
            sums[side] = term if sums[side] is None else sums[side] + term
        first, second = merged(*sums)
        fine = jnp.concatenate([first.astype(BF16), second.astype(BF16)], axis=1)
        terms.append(jnp.dot(restrict_ref[half], fine, preferred_element_type=F32))
    own_out[...] = terms[0][B:] + terms[1][:B]
    before_out[...] = placed(terms[0][:B], True).astype(BF16)
    after_out[...] = placed(terms[1][B:], True).astype(BF16)


def inner_kernel(index_ref, slots_ref, odd_ref, even_ref, edge_ref, sums_ref, band):
    turn = 0
    for n, near in enumerate((odd_ref, even_ref)):
        s = plane_of(1 - n)
        for half in range(2):
            sums = [None, None]
            for j in range(3):
                part = half + j
                if part in (0, 3):
                    gather(index_ref, slots_ref, s, half, j, edge_ref.at[2 * n + half])
                    continue
                turn = (turn + 1) % 3
                gather(index_ref, slots_ref, s, half, j, band.at[turn])
                sums[part // 2] = jnp.dot(
                    band[turn], rows_of(near, (part - 1) * HALF), preferred_element_type=F32
                )
            first, second = merged(*sums)
            sums_ref[n, half, :, :PAIR] = first
            sums_ref[n, half, :, PAIR:] = second


def outer_kernel(
    edge_ref, sums_ref, restrict_ref, left_ref, right_ref, own_mid, before_mid, after_mid,
    own_ref, before_ref, after_ref
):
    lower = lax.broadcasted_iota(jnp.int32, (DEPTH, PAIR), 1) < B
    mid = slice(2 * PAIR, 4 * PAIR)
    own_ref[:, mid] = own_mid[...]
    before_ref[:, mid] = before_mid[...]
    after_ref[:, mid] = after_mid[...]
    for n in range(2):
        terms = []
        for half in range(2):
            first, second = sums_ref[n, half, :, :PAIR], sums_ref[n, half, :, PAIR:]
            against = rows_of(right_ref if half else left_ref, n * HALF)
            if half:
                against = swap_lanes(against)
            term = jnp.dot(edge_ref[2 * n + half], against, preferred_element_type=F32)
            if half:
                first = first + jnp.where(lower, 0.0, term)
                second = second + jnp.where(lower, term, 0.0)
            else:
                first = first + term
            fine = jnp.concatenate([first.astype(BF16), second.astype(BF16)], axis=1)
            terms.append(jnp.dot(restrict_ref[half], fine, preferred_element_type=F32))
        cols = pl.ds(pl.multiple_of(plane_of(1 - n) * 2 * PAIR, PAIR), 2 * PAIR)
        own_ref[:, cols] = placed(terms[0][B:] + terms[1][:B], True)
        before_ref[:, cols] = terms[0][:B].astype(BF16)
        after_ref[:, cols] = terms[1][B:].astype(BF16)


OWN_AT = (0, 1, 3, 4, 5, 6)
ABOVE_AT = (1, 2, 3, 4, 6, 7)
BELOW_AT = (0, 1, 2, 3, 5, 6)


def join_kernel(own_ref, above_ref, below_ref, out_ref):
    for tile in range(8):
        width = PAIR if tile < 7 else B
        total = None
        for ref, places in ((own_ref, OWN_AT), (above_ref, ABOVE_AT), (below_ref, BELOW_AT)):
            if tile in places:
                at = places.index(tile) * PAIR
                piece = ref[:, at : at + width].astype(F32)
                total = piece if total is None else total + piece
        out_ref[0, :, tile * PAIR : tile * PAIR + width] = total


def in_hbm(x):
    return pltpu.with_memory_space_constraint(x, pltpu.HBM)


def whole(count):
    return [pl.BlockSpec(memory_space=pltpu.VMEM)] * count


def slot_table(a_cols, a_count):
    first_block = lax.axis_index("col") * AGG
    local_q = jnp.arange(AGG, dtype=jnp.int32)[:, None]
    reach = (a_cols[0] % PLANE - first_block + HALF) % PLANE - HALF * (local_q // HALF)
    place = a_cols[0] // PLANE * SPAN + reach
    slot = jnp.arange(KA, dtype=jnp.int32)
    live = slot[None, :] < a_count[0][:, None]
    dest = jnp.arange(3 * SPAN, dtype=jnp.int32)
    hit = (place[:, :, None] == dest) & live[:, :, None]
    entry = slot[:, None] // 2 + TILES * ((slot[:, None] + dest[None, :]) % 2)
    return EMPTY + jnp.sum(jnp.where(hit, entry[None] - EMPTY, 0), axis=1)


def body(a_vals, a_cols, a_count, p_vals, p_cols, r_vals, r_cols):
    own, head, tail = order(p_vals, p_cols)
    odd = swap_rows(own, 1)
    even = swap_rows(own, 0)
    left = shift_cols(tail, 1)
    right = shift_cols(head, -1)
    index = slot_table(a_cols, a_count).reshape(-1)
    slots, restrict = prepare(r_cols, a_vals, r_vals)
    odd, even, left, right, restrict, index = lax.optimization_barrier((odd, even, left, right, restrict, index))
    smem = pl.BlockSpec(memory_space=pltpu.SMEM)
    band = pltpu.VMEM((3, DEPTH, DEPTH), BF16)
    own_mid, before_mid, after_mid = pl.pallas_call(
        middle_kernel,
        out_shape=(
            jax.ShapeDtypeStruct((B, 2 * PAIR), F32),
            jax.ShapeDtypeStruct((B, 2 * PAIR), BF16),
            jax.ShapeDtypeStruct((B, 2 * PAIR), BF16),
        ),
        in_specs=[smem] + whole(5),
        out_specs=tuple(whole(3)),
        scratch_shapes=[band],
        compiler_params=pltpu.CompilerParams(vmem_limit_bytes=16 << 20),
        cost_estimate=pl.CostEstimate(flops=1 << 30, bytes_accessed=4 << 20, transcendentals=0),
        name="middle",
    )(index, slots, restrict, left, own, right)
    both_left = shift_cols(jnp.concatenate([odd[HALF:], even[HALF:]], axis=0), 1)
    both_right = shift_cols(jnp.concatenate([odd[:HALF], even[:HALF]], axis=0), -1)

    edge, sums = pl.pallas_call(
        inner_kernel,
        out_shape=(
            jax.ShapeDtypeStruct((4, DEPTH, DEPTH), BF16),
            jax.ShapeDtypeStruct((2, 2, DEPTH, 2 * PAIR), F32),
        ),
        in_specs=[smem] + whole(3),
        out_specs=tuple(whole(2)),
        scratch_shapes=[band],
        compiler_params=pltpu.CompilerParams(vmem_limit_bytes=16 << 20),
        cost_estimate=pl.CostEstimate(flops=1 << 30, bytes_accessed=8 << 20, transcendentals=0),
        name="inner",
    )(index, slots, odd, even)
    owned, before, after = pl.pallas_call(
        outer_kernel,
        out_shape=(
            jax.ShapeDtypeStruct((B, 6 * PAIR), F32),
            jax.ShapeDtypeStruct((B, 6 * PAIR), BF16),
            jax.ShapeDtypeStruct((B, 6 * PAIR), BF16),
        ),
        in_specs=whole(8),
        out_specs=tuple(whole(3)),
        compiler_params=pltpu.CompilerParams(vmem_limit_bytes=12 << 20),
        cost_estimate=pl.CostEstimate(flops=1 << 30, bytes_accessed=4 << 20, transcendentals=0),
        name="outer",
    )(edge, sums, restrict, both_left, both_right, own_mid, before_mid, after_mid)
    above = shift_cols(before, -1)
    below = shift_cols(after, 1)
    return pl.pallas_call(
        join_kernel,
        out_shape=jax.ShapeDtypeStruct((1, B, 15 * B), F32),
        in_specs=whole(3),
        out_specs=whole(1)[0],
        compiler_params=pltpu.CompilerParams(vmem_limit_bytes=4 << 20),
        name="join",
    )(owned, above, below)


def solution(mesh):
    return jax.shard_map(
        body,
        mesh=mesh,
        in_specs=(
            P("row", "col", None, None),
            P("row", "col", None),
            P("row", "col"),
            P("row", "col", None, None),
            P("row", "col", None),
            P("row", "col", None, None),
            P("row", "col", None),
        ),
        out_specs=P("row", "col", None),
        check_vma=False,
    )
```

```python
import jax
import jax.numpy as jnp
from jax import lax
from jax.experimental import pallas as pl
from jax.experimental.pallas import tpu as pltpu
from jax.sharding import PartitionSpec as P

PLANE = 256
AGG = 16
HALF = 8
B = 64
KA = 32
PAIR = 2 * B
TILES = KA // 2
EMPTY = 2 * TILES
SPAN = 24
DEPTH = HALF * B

F32 = jnp.float32
BF16 = jnp.bfloat16


def shift_cols(value, step):
    count = lax.axis_size("col")
    return lax.ppermute(value, "col", [(i, (i + step) % count) for i in range(count)])


def swap_rows(value, first):
    pairs = []
    for row in range(first, lax.axis_size("row") - 1, 2):
        pairs += [(row, row + 1), (row + 1, row)]
    return lax.ppermute(value, "row", pairs)


def plane_of(first):
    return 2 * lax.rem(lax.axis_index("row") + first + 1, 2)


def swap_lanes(x):
    return pltpu.roll(x, B, 1)


def flip_mask(cols_ref, q):
    first_own = cols_ref[0:1, q : q + 1] == lax.axis_index("col")
    value = jnp.where(first_own, 1.0, 0.0) if q < HALF else jnp.where(first_own, 0.0, 1.0)
    return jnp.broadcast_to(value, (B, PAIR)) > 0.5


def ordered(x, cols_ref, q):
    return jnp.where(flip_mask(cols_ref, q), swap_lanes(x), x)


def order_kernel(cols_hbm, p_hbm, all_ref, head_ref, tail_ref, cols_ref, raw, sems):
    parts = 4
    size = AGG // parts
    cols_copy = pltpu.make_async_copy(cols_hbm, cols_ref, sems.at[parts])
    cols_copy.start()

    def fetch(part):
        at = pl.ds(part * size, size)
        return pltpu.make_async_copy(p_hbm.at[0, at], raw.at[at], sems.at[part])

    for part in range(parts):
        fetch(part).start()
    cols_copy.wait()
    for part in range(parts):
        fetch(part).wait()
        for q in range(part * size, (part + 1) * size):
            y = ordered(raw[q], cols_ref, q)
            all_ref[q] = y
            if q < HALF:
                head_ref[q] = y
            else:
                tail_ref[q - HALF] = y


def order(p_vals, p_cols):
    half = jax.ShapeDtypeStruct((HALF, B, PAIR), BF16)
    return pl.pallas_call(
        order_kernel,
        out_shape=(jax.ShapeDtypeStruct((AGG, B, PAIR), BF16), half, half),
        in_specs=[pl.BlockSpec(memory_space=pl.ANY)] * 2,
        out_specs=tuple(whole(3)),
        scratch_shapes=[
            pltpu.VMEM((2, AGG), jnp.int32),
            pltpu.VMEM((AGG, B, PAIR), BF16),
            pltpu.SemaphoreType.DMA((5,)),
        ],
        compiler_params=pltpu.CompilerParams(vmem_limit_bytes=4 << 20),
        name="order",
    )(in_hbm(p_cols[0].T), in_hbm(p_vals))


def slot_table(cols, count_ref, wide_ref, table_ref):
    row = lax.broadcasted_iota(jnp.int32, (AGG, KA), 0)
    reach = ((cols & (PLANE - 1)) - lax.axis_index("col") * AGG + HALF) & (PLANE - 1)
    wide_ref[:AGG, :KA] = (cols // PLANE) * SPAN + reach - jnp.where(row < HALF, 0, HALF)
    places = wide_ref[...].T
    slot = lax.broadcasted_iota(jnp.int32, (KA, PAIR), 0)
    dest = lax.broadcasted_iota(jnp.int32, (KA, PAIR), 1)
    entry = slot // 2 + TILES * ((slot + dest) & 1) - EMPTY
    for q in range(AGG):
        place = jnp.broadcast_to(places[:KA, q : q + 1], (KA, PAIR))
        count = jnp.broadcast_to(count_ref[0:1, q : q + 1], (KA, PAIR))
        found = jnp.where((place == dest) & (slot < count), entry, 0)
        table_ref[q : q + 1, :] = EMPTY + jnp.sum(found, axis=0, keepdims=True)


def prepare_kernel(
    links_hbm, count_hbm, cols_hbm, a_hbm, r_hbm, links_ref, count_ref, slots_ref, restrict_ref,
    cols_ref, raw, sems, small_sems
):
    def fetch(q):
        return pltpu.make_async_copy(a_hbm.at[0, q], slots_ref.at[q, :, pl.ds(0, KA * B)], sems.at[q])

    small = [
        pltpu.make_async_copy(cols_hbm, cols_ref, small_sems.at[0]),
        pltpu.make_async_copy(r_hbm.at[0], raw, small_sems.at[1]),
        pltpu.make_async_copy(links_hbm.at[0], links_ref, small_sems.at[2]),
        pltpu.make_async_copy(count_hbm, count_ref, small_sems.at[3]),
    ]
    for copy in small:
        copy.start()
    for q in range(AGG):
        fetch(q).start()
    for copy in small:
        copy.wait()
    for q in range(0, AGG, 2):
        two = jnp.concatenate([ordered(raw[q], cols_ref, q), ordered(raw[q + 1], cols_ref, q + 1)], axis=0)
        at = (q % HALF) * B
        restrict_ref[q // HALF, :, at : at + PAIR] = two.T

    def row(q, carry):
        slots_ref[q, :, EMPTY * PAIR :] = jnp.zeros((B, PAIR), BF16)
        fetch(q).wait()
        for k in range(TILES):
            x = slots_ref[q, :, k * PAIR : (k + 1) * PAIR]
            slots_ref[q, :, (TILES + k) * PAIR : (TILES + k + 1) * PAIR] = swap_lanes(x)
        return carry

    lax.fori_loop(0, AGG, row, 0)


def prepare(a_cols, a_count, r_cols, a_vals, r_vals):
    return pl.pallas_call(
        prepare_kernel,
        out_shape=(
            jax.ShapeDtypeStruct((AGG, KA), jnp.int32),
            jax.ShapeDtypeStruct((1, AGG), jnp.int32),
            pltpu.VMEM((AGG, B, (EMPTY + 1) * PAIR), BF16),
            jax.ShapeDtypeStruct((2, PAIR, DEPTH), BF16),
        ),
        in_specs=[pl.BlockSpec(memory_space=pl.ANY)] * 5,
        out_specs=tuple(whole(4)),
        scratch_shapes=[
            pltpu.VMEM((2, AGG), jnp.int32),
            pltpu.VMEM((AGG, B, PAIR), BF16),
            pltpu.SemaphoreType.DMA((AGG,)),
            pltpu.SemaphoreType.DMA((4,)),
        ],
        compiler_params=pltpu.CompilerParams(vmem_limit_bytes=12 << 20),
        cost_estimate=pl.CostEstimate(flops=0, bytes_accessed=6 << 20, transcendentals=0),
        name="prepare",
    )(in_hbm(a_cols), in_hbm(a_count), in_hbm(r_cols[0].T), in_hbm(a_vals), in_hbm(r_vals))


def placed(x, shifted):
    if not shifted:
        return x
    lower = lax.broadcasted_iota(jnp.int32, (B, PAIR), 1) < B
    first, second = swap_lanes(x[:, :PAIR]), swap_lanes(x[:, PAIR:])
    return jnp.concatenate([jnp.where(lower, 0.0, first), jnp.where(lower, first, second)], axis=1)


def banded(blocks_ref, against, j):
    mid = DEPTH // 2

    def part(rows, depth):
        return jnp.dot(blocks_ref[rows, depth], against[depth], preferred_element_type=F32)

    everything, first, second = slice(0, DEPTH), slice(0, mid), slice(mid, DEPTH)
    if j == 1:
        return part(everything, everything)
    if j == 0:
        return jnp.concatenate([part(first, everything), part(second, second)], axis=0)
    return jnp.concatenate([part(first, first), part(second, everything)], axis=0)


def merged(low, high):
    lower = lax.broadcasted_iota(jnp.int32, (DEPTH, PAIR), 1) < B
    high = swap_lanes(high)
    return low + jnp.where(lower, 0.0, high), jnp.where(lower, high, 0.0)


def rows_of(ref, start):
    return ref[start : start + HALF].reshape(DEPTH, PAIR)


def gather(index_ref, slots_ref, s, half, j, into):
    lower = lax.broadcasted_iota(jnp.int32, (B, PAIR), 1) < B
    for e in range(HALF):
        q = half * HALF + e
        at = s * SPAN + j * HALF
        for tile in range(HALF // 2):
            rows, cols = slice(e * B, (e + 1) * B), slice(tile * PAIR, (tile + 1) * PAIR)
            if (j == 0 and tile < e // 2) or (j == 2 and tile > e // 2):
                early, near = e < HALF // 2, tile < HALF // 4
                if (j == 0 and (early or not near)) or (j == 2 and (near or not early)):
                    into[rows, cols] = jnp.zeros((B, PAIR), BF16)
                continue
            first = pl.multiple_of(index_ref[q, at + 2 * tile] * PAIR, PAIR)
            second = pl.multiple_of(index_ref[q, at + 2 * tile + 1] * PAIR, PAIR)
            into[rows, cols] = jnp.where(
                lower, slots_ref[q, :, pl.ds(first, PAIR)], slots_ref[q, :, pl.ds(second, PAIR)]
            )


def products_kernel(
    links_ref, count_ref, slots_ref, restrict_ref, left_ref, own_ref, right_ref, odd_ref, even_ref,
    edge_ref, sums_ref, own_out, before_out, after_out, index_ref, wide_ref, table_ref, band, sem
):
    slot_table(links_ref[...], count_ref, wide_ref, table_ref)
    to_scalars = pltpu.make_async_copy(table_ref, index_ref, sem)
    to_scalars.start()
    to_scalars.wait()

    turn = 0
    terms = []
    for n, near in ((2, own_ref), (0, odd_ref), (1, even_ref)):
        s = 1 if n == 2 else plane_of(1 - n)
        for half in range(2):
            sums = [None, None]
            for j in range(3):
                part = half + j
                if part in (0, 3) and n < 2:
                    gather(index_ref, slots_ref, s, half, j, edge_ref.at[2 * n + half])
                    continue
                if part in (0, 3):
                    against = rows_of(right_ref if part else left_ref, 0)
                else:
                    against = rows_of(near, (part - 1) * HALF)
                turn = (turn + 1) % 3
                gather(index_ref, slots_ref, s, half, j, band.at[turn])
                term = banded(band.at[turn], against, j)
                sums[part // 2] = term if sums[part // 2] is None else sums[part // 2] + term
            first, second = merged(*sums)
            if n < 2:
                sums_ref[n, half, :, :PAIR] = first
                sums_ref[n, half, :, PAIR:] = second
            else:
                fine = jnp.concatenate([first.astype(BF16), second.astype(BF16)], axis=1)
                terms.append(jnp.dot(restrict_ref[half], fine, preferred_element_type=F32))
    own_out[...] = terms[0][B:] + terms[1][:B]
    before_out[...] = placed(terms[0][:B], True).astype(BF16)
    after_out[...] = placed(terms[1][B:], True).astype(BF16)


def outer_kernel(
    edge_ref, sums_ref, restrict_ref, left_ref, right_ref, own_mid, before_mid, after_mid,
    own_ref, before_ref, after_ref
):
    lower = lax.broadcasted_iota(jnp.int32, (DEPTH, PAIR), 1) < B
    mid = slice(2 * PAIR, 4 * PAIR)
    own_ref[:, mid] = own_mid[...]
    before_ref[:, mid] = before_mid[...]
    after_ref[:, mid] = after_mid[...]
    for n in range(2):
        terms = []
        for half in range(2):
            first, second = sums_ref[n, half, :, :PAIR], sums_ref[n, half, :, PAIR:]
            against = rows_of(right_ref if half else left_ref, n * HALF)
            if half:
                against = swap_lanes(against)
            term = banded(edge_ref.at[2 * n + half], against, 2 * half)
            if half:
                first = first + jnp.where(lower, 0.0, term)
                second = second + jnp.where(lower, term, 0.0)
            else:
                first = first + term
            fine = jnp.concatenate([first.astype(BF16), second.astype(BF16)], axis=1)
            terms.append(jnp.dot(restrict_ref[half], fine, preferred_element_type=F32))
        cols = pl.ds(pl.multiple_of(plane_of(1 - n) * 2 * PAIR, PAIR), 2 * PAIR)
        own_ref[:, cols] = placed(terms[0][B:] + terms[1][:B], True)
        before_ref[:, cols] = terms[0][:B].astype(BF16)
        after_ref[:, cols] = terms[1][B:].astype(BF16)


OWN_AT = (0, 1, 3, 4, 5, 6)
ABOVE_AT = (1, 2, 3, 4, 6, 7)
BELOW_AT = (0, 1, 2, 3, 5, 6)


def join_kernel(own_ref, below_ref, above_ref, out_ref):
    for tile in range(8):
        width = PAIR if tile < 7 else B
        total = None
        for ref, places in ((own_ref, OWN_AT), (above_ref, ABOVE_AT), (below_ref, BELOW_AT)):
            if tile in places:
                at = places.index(tile) * PAIR
                piece = ref[:, at : at + width].astype(F32)
                total = piece if total is None else total + piece
        out_ref[0, :, tile * PAIR : tile * PAIR + width] = total


def in_hbm(x):
    return pltpu.with_memory_space_constraint(x, pltpu.HBM)


def whole(count):
    return [pl.BlockSpec(memory_space=pltpu.VMEM)] * count


def body(a_vals, a_cols, a_count, p_vals, p_cols, r_vals, r_cols):
    own, head, tail = order(p_vals, p_cols)
    odd = swap_rows(own, 1)
    even = swap_rows(own, 0)
    left = shift_cols(tail, 1)
    right = shift_cols(head, -1)
    links, count, slots, restrict = prepare(a_cols, a_count, r_cols, a_vals, r_vals)
    even, odd, left, right, slots = lax.optimization_barrier((even, odd, left, right, slots))
    both_left = shift_cols(jnp.concatenate([odd[HALF:], even[HALF:]], axis=0), 1)
    both_right = shift_cols(jnp.concatenate([odd[:HALF], even[:HALF]], axis=0), -1)

    edge, sums, own_mid, before_mid, after_mid = pl.pallas_call(
        products_kernel,
        out_shape=(
            jax.ShapeDtypeStruct((4, DEPTH, DEPTH), BF16),
            jax.ShapeDtypeStruct((2, 2, DEPTH, 2 * PAIR), F32),
            jax.ShapeDtypeStruct((B, 2 * PAIR), F32),
            jax.ShapeDtypeStruct((B, 2 * PAIR), BF16),
            jax.ShapeDtypeStruct((B, 2 * PAIR), BF16),
        ),
        in_specs=whole(9),
        out_specs=tuple(whole(5)),
        scratch_shapes=[
            pltpu.SMEM((AGG, PAIR), jnp.int32),
            pltpu.VMEM((PAIR, PAIR), jnp.int32),
            pltpu.VMEM((AGG, PAIR), jnp.int32),
            pltpu.VMEM((3, DEPTH, DEPTH), BF16),
            pltpu.SemaphoreType.DMA,
        ],
        compiler_params=pltpu.CompilerParams(vmem_limit_bytes=20 << 20),
        cost_estimate=pl.CostEstimate(flops=2 << 30, bytes_accessed=8 << 20, transcendentals=0),
        name="products",
    )(links, count, slots, restrict, left, own, right, odd, even)
    owned, before, after = pl.pallas_call(
        outer_kernel,
        out_shape=(
            jax.ShapeDtypeStruct((B, 6 * PAIR), F32),
            jax.ShapeDtypeStruct((B, 6 * PAIR), BF16),
            jax.ShapeDtypeStruct((B, 6 * PAIR), BF16),
        ),
        in_specs=whole(8),
        out_specs=tuple(whole(3)),
        compiler_params=pltpu.CompilerParams(vmem_limit_bytes=12 << 20),
        cost_estimate=pl.CostEstimate(flops=1 << 30, bytes_accessed=4 << 20, transcendentals=0),
        name="outer",
    )(edge, sums, restrict, both_left, both_right, own_mid, before_mid, after_mid)
    below = shift_cols(after, 1)
    above = shift_cols(before, -1)
    return pl.pallas_call(
        join_kernel,
        out_shape=jax.ShapeDtypeStruct((1, B, 15 * B), F32),
        in_specs=whole(3),
        out_specs=whole(1)[0],
        compiler_params=pltpu.CompilerParams(vmem_limit_bytes=4 << 20),
        name="join",
    )(owned, below, above)


def solution(mesh):
    return jax.shard_map(
        body,
        mesh=mesh,
        in_specs=(
            P("row", "col", None, None),
            P("row", "col", None),
            P("row", "col"),
            P("row", "col", None, None),
            P("row", "col", None),
            P("row", "col", None, None),
            P("row", "col", None),
        ),
        out_specs=P("row", "col", None),
        check_vma=False,
    )
```

```python
import jax
import jax.numpy as jnp
from jax import lax
from jax.experimental import pallas as pl
from jax.experimental.pallas import tpu as pltpu
from jax.sharding import PartitionSpec as P

PLANE = 256
AGG = 16
HALF = 8
B = 64
KA = 32
PAIR = 2 * B
TILES = KA // 2
EMPTY = 2 * TILES
SPAN = 24
DEPTH = HALF * B

F32 = jnp.float32
BF16 = jnp.bfloat16


def shift_cols(value, step):
    count = lax.axis_size("col")
    return lax.ppermute(value, "col", [(i, (i + step) % count) for i in range(count)])


def swap_rows(value, first):
    pairs = []
    for row in range(first, lax.axis_size("row") - 1, 2):
        pairs += [(row, row + 1), (row + 1, row)]
    return lax.ppermute(value, "row", pairs)


def plane_of(first):
    return 2 * lax.rem(lax.axis_index("row") + first + 1, 2)


def swap_lanes(x):
    return pltpu.roll(x, B, 1)


def flip_mask(cols_ref, q):
    first_own = cols_ref[0:1, q : q + 1] == lax.axis_index("col")
    value = jnp.where(first_own, 1.0, 0.0) if q < HALF else jnp.where(first_own, 0.0, 1.0)
    return jnp.broadcast_to(value, (B, PAIR)) > 0.5


def ordered(x, cols_ref, q):
    return jnp.where(flip_mask(cols_ref, q), swap_lanes(x), x)


def order_kernel(cols_hbm, p_hbm, all_ref, head_ref, tail_ref, cols_ref, raw, sems):
    parts = 2
    size = AGG // parts
    cols_copy = pltpu.make_async_copy(cols_hbm, cols_ref, sems.at[parts])
    cols_copy.start()

    def fetch(part):
        at = pl.ds(part * size, size)
        return pltpu.make_async_copy(p_hbm.at[0, at], raw.at[at], sems.at[part])

    for part in range(parts):
        fetch(part).start()
    cols_copy.wait()
    for part in range(parts):
        fetch(part).wait()
        for q in range(part * size, (part + 1) * size):
            y = ordered(raw[q], cols_ref, q)
            all_ref[q] = y
            if q < HALF:
                head_ref[q] = y
            else:
                tail_ref[q - HALF] = y


def order(p_vals, p_cols):
    half = jax.ShapeDtypeStruct((HALF, B, PAIR), BF16)
    return pl.pallas_call(
        order_kernel,
        out_shape=(jax.ShapeDtypeStruct((AGG, B, PAIR), BF16), half, half),
        in_specs=[pl.BlockSpec(memory_space=pl.ANY)] * 2,
        out_specs=tuple(whole(3)),
        scratch_shapes=[
            pltpu.VMEM((2, AGG), jnp.int32),
            pltpu.VMEM((AGG, B, PAIR), BF16),
            pltpu.SemaphoreType.DMA((3,)),
        ],
        compiler_params=pltpu.CompilerParams(vmem_limit_bytes=4 << 20),
        name="order",
    )(in_hbm(p_cols[0].T), in_hbm(p_vals))


def slot_table(cols, count_ref, wide_ref, table_ref):
    row = lax.broadcasted_iota(jnp.int32, (AGG, KA), 0)
    reach = ((cols & (PLANE - 1)) - lax.axis_index("col") * AGG + HALF) & (PLANE - 1)
    wide_ref[:AGG, :KA] = (cols // PLANE) * SPAN + reach - jnp.where(row < HALF, 0, HALF)
    places = wide_ref[...].T
    slot = lax.broadcasted_iota(jnp.int32, (KA, PAIR), 0)
    dest = lax.broadcasted_iota(jnp.int32, (KA, PAIR), 1)
    entry = slot // 2 + TILES * ((slot + dest) & 1) - EMPTY
    for q in range(AGG):
        place = jnp.broadcast_to(places[:KA, q : q + 1], (KA, PAIR))
        count = jnp.broadcast_to(count_ref[0:1, q : q + 1], (KA, PAIR))
        found = jnp.where((place == dest) & (slot < count), entry, 0)
        table_ref[q : q + 1, :] = EMPTY + jnp.sum(found, axis=0, keepdims=True)


def prepare_kernel(
    links_hbm, count_hbm, cols_hbm, a_hbm, r_hbm, index_ref, slots_ref, restrict_ref,
    links_ref, count_ref, cols_ref, wide_ref, table_ref, raw, sems, small_sems
):
    def fetch(q):
        return pltpu.make_async_copy(a_hbm.at[0, q], slots_ref.at[q, :, pl.ds(0, KA * B)], sems.at[q])

    small = [
        pltpu.make_async_copy(cols_hbm, cols_ref, small_sems.at[0]),
        pltpu.make_async_copy(r_hbm.at[0], raw, small_sems.at[1]),
        pltpu.make_async_copy(links_hbm.at[0], links_ref, small_sems.at[2]),
        pltpu.make_async_copy(count_hbm, count_ref, small_sems.at[3]),
    ]
    for q in range(AGG):
        fetch(q).start()
    for copy in small:
        copy.start(priority=1)
    def row(q, carry):
        slots_ref[q, :, EMPTY * PAIR :] = jnp.zeros((B, PAIR), BF16)
        fetch(q).wait()
        for k in range(TILES):
            x = slots_ref[q, :, k * PAIR : (k + 1) * PAIR]
            slots_ref[q, :, (TILES + k) * PAIR : (TILES + k + 1) * PAIR] = swap_lanes(x)
        return carry

    lax.fori_loop(0, AGG, row, 0)
    for copy in small:
        copy.wait()
    slot_table(links_ref[...], count_ref, wide_ref, table_ref)
    to_scalars = pltpu.make_async_copy(table_ref, index_ref, small_sems.at[4])
    to_scalars.start()
    unit = jnp.where(
        lax.broadcasted_iota(jnp.int32, (PAIR, PAIR), 0) == lax.broadcasted_iota(jnp.int32, (PAIR, PAIR), 1), 1.0, 0.0
    ).astype(BF16)
    for q in range(0, AGG, 2):
        two = jnp.concatenate([ordered(raw[q], cols_ref, q), ordered(raw[q + 1], cols_ref, q + 1)], axis=0)
        at = (q % HALF) * B
        turned = lax.dot_general(unit, two, (((1,), (1,)), ((), ())), preferred_element_type=F32)
        restrict_ref[q // HALF, :, at : at + PAIR] = turned.astype(BF16)

    to_scalars.wait()


def prepare(a_cols, a_count, r_cols, a_vals, r_vals):
    return pl.pallas_call(
        prepare_kernel,
        out_shape=(
            pltpu.SMEM((AGG, PAIR), jnp.int32),
            pltpu.VMEM((AGG, B, (EMPTY + 1) * PAIR), BF16),
            jax.ShapeDtypeStruct((2, PAIR, DEPTH), BF16),
        ),
        in_specs=[pl.BlockSpec(memory_space=pl.ANY)] * 5,
        out_specs=(pl.BlockSpec(memory_space=pltpu.SMEM), *whole(2)),
        scratch_shapes=[
            pltpu.VMEM((AGG, KA), jnp.int32),
            pltpu.VMEM((1, AGG), jnp.int32),
            pltpu.VMEM((2, AGG), jnp.int32),
            pltpu.VMEM((PAIR, PAIR), jnp.int32),
            pltpu.VMEM((AGG, PAIR), jnp.int32),
            pltpu.VMEM((AGG, B, PAIR), BF16),
            pltpu.SemaphoreType.DMA((AGG,)),
            pltpu.SemaphoreType.DMA((5,)),
        ],
        compiler_params=pltpu.CompilerParams(vmem_limit_bytes=12 << 20),
        cost_estimate=pl.CostEstimate(flops=0, bytes_accessed=6 << 20, transcendentals=0),
        name="prepare",
    )(in_hbm(a_cols), in_hbm(a_count), in_hbm(r_cols[0].T), in_hbm(a_vals), in_hbm(r_vals))


def placed(x, shifted):
    if not shifted:
        return x
    lower = lax.broadcasted_iota(jnp.int32, (B, PAIR), 1) < B
    first, second = swap_lanes(x[:, :PAIR]), swap_lanes(x[:, PAIR:])
    return jnp.concatenate([jnp.where(lower, 0.0, first), jnp.where(lower, first, second)], axis=1)


def banded(blocks_ref, against, j):
    mid = DEPTH // 2

    def part(rows, depth):
        return jnp.dot(blocks_ref[rows, depth], against[depth], preferred_element_type=F32)

    everything, first, second = slice(0, DEPTH), slice(0, mid), slice(mid, DEPTH)
    if j == 1:
        return part(everything, everything)
    if j == 0:
        return jnp.concatenate([part(first, everything), part(second, second)], axis=0)
    return jnp.concatenate([part(first, first), part(second, everything)], axis=0)


def merged(low, high):
    lower = lax.broadcasted_iota(jnp.int32, (DEPTH, PAIR), 1) < B
    high = swap_lanes(high)
    return low + jnp.where(lower, 0.0, high), jnp.where(lower, high, 0.0)


def rows_of(ref, start):
    return ref[start : start + HALF].reshape(DEPTH, PAIR)


def gather(index_ref, slots_ref, s, half, j, into):
    lower = lax.broadcasted_iota(jnp.int32, (B, PAIR), 1) < B
    for e in range(HALF):
        q = half * HALF + e
        at = s * SPAN + j * HALF
        for tile in range(HALF // 2):
            rows, cols = slice(e * B, (e + 1) * B), slice(tile * PAIR, (tile + 1) * PAIR)
            if (j == 0 and tile < e // 2) or (j == 2 and tile > e // 2):
                early, near = e < HALF // 2, tile < HALF // 4
                if (j == 0 and (early or not near)) or (j == 2 and (near or not early)):
                    into[rows, cols] = jnp.zeros((B, PAIR), BF16)
                continue
            first = pl.multiple_of(index_ref[q, at + 2 * tile] * PAIR, PAIR)
            second = pl.multiple_of(index_ref[q, at + 2 * tile + 1] * PAIR, PAIR)
            into[rows, cols] = jnp.where(
                lower, slots_ref[q, :, pl.ds(first, PAIR)], slots_ref[q, :, pl.ds(second, PAIR)]
            )


def products_kernel(
    index_ref, slots_ref, restrict_ref, left_ref, own_ref, right_ref, odd_ref, even_ref,
    edge_ref, sums_ref, own_out, before_out, after_out, band
):
    turn = 0
    terms = []
    for n, near in ((2, own_ref), (0, odd_ref), (1, even_ref)):
        s = 1 if n == 2 else plane_of(1 - n)
        for half in range(2):
            sums = [None, None]
            for j in range(3):
                part = half + j
                if part in (0, 3) and n < 2:
                    gather(index_ref, slots_ref, s, half, j, edge_ref.at[2 * n + half])
                    continue
                if part in (0, 3):
                    against = rows_of(right_ref if part else left_ref, 0)
                else:
                    against = rows_of(near, (part - 1) * HALF)
                turn = (turn + 1) % 3
                gather(index_ref, slots_ref, s, half, j, band.at[turn])
                term = banded(band.at[turn], against, j)
                sums[part // 2] = term if sums[part // 2] is None else sums[part // 2] + term
            first, second = merged(*sums)
            if n < 2:
                sums_ref[n, half, :, :PAIR] = first
                sums_ref[n, half, :, PAIR:] = second
            else:
                fine = jnp.concatenate([first.astype(BF16), second.astype(BF16)], axis=1)
                terms.append(jnp.dot(restrict_ref[half], fine, preferred_element_type=F32))
    own_out[...] = terms[0][B:] + terms[1][:B]
    before_out[...] = placed(terms[0][:B], True).astype(BF16)
    after_out[...] = placed(terms[1][B:], True).astype(BF16)


def outer_kernel(
    edge_ref, sums_ref, restrict_ref, left_ref, right_ref, own_mid, before_mid, after_mid,
    own_ref, before_ref, after_ref
):
    lower = lax.broadcasted_iota(jnp.int32, (DEPTH, PAIR), 1) < B
    mid = slice(2 * PAIR, 4 * PAIR)
    own_ref[:, mid] = own_mid[...]
    before_ref[:, mid] = before_mid[...]
    after_ref[:, mid] = after_mid[...]
    for n in range(2):
        terms = []
        for half in range(2):
            first, second = sums_ref[n, half, :, :PAIR], sums_ref[n, half, :, PAIR:]
            against = rows_of(right_ref if half else left_ref, n * HALF)
            if half:
                against = swap_lanes(against)
            term = banded(edge_ref.at[2 * n + half], against, 2 * half)
            if half:
                first = first + jnp.where(lower, 0.0, term)
                second = second + jnp.where(lower, term, 0.0)
            else:
                first = first + term
            fine = jnp.concatenate([first.astype(BF16), second.astype(BF16)], axis=1)
            terms.append(jnp.dot(restrict_ref[half], fine, preferred_element_type=F32))
        cols = pl.ds(pl.multiple_of(plane_of(1 - n) * 2 * PAIR, PAIR), 2 * PAIR)
        own_ref[:, cols] = placed(terms[0][B:] + terms[1][:B], True)
        before_ref[:, cols] = terms[0][:B].astype(BF16)
        after_ref[:, cols] = terms[1][B:].astype(BF16)


OWN_AT = (0, 1, 3, 4, 5, 6)
ABOVE_AT = (1, 2, 3, 4, 6, 7)
BELOW_AT = (0, 1, 2, 3, 5, 6)


def join_kernel(own_ref, below_ref, above_ref, out_ref):
    for tile in range(8):
        width = PAIR if tile < 7 else B
        total = None
        for ref, places in ((own_ref, OWN_AT), (above_ref, ABOVE_AT), (below_ref, BELOW_AT)):
            if tile in places:
                at = places.index(tile) * PAIR
                piece = ref[:, at : at + width].astype(F32)
                total = piece if total is None else total + piece
        out_ref[0, :, tile * PAIR : tile * PAIR + width] = total


def in_hbm(x):
    return pltpu.with_memory_space_constraint(x, pltpu.HBM)


def whole(count):
    return [pl.BlockSpec(memory_space=pltpu.VMEM)] * count


def body(a_vals, a_cols, a_count, p_vals, p_cols, r_vals, r_cols):
    own, head, tail = order(p_vals, p_cols)
    odd = swap_rows(own, 1)
    even = swap_rows(own, 0)
    left = shift_cols(tail, 1)
    right = shift_cols(head, -1)
    index, slots, restrict = prepare(a_cols, a_count, r_cols, a_vals, r_vals)
    even, odd, left, right, slots = lax.optimization_barrier((even, odd, left, right, slots))
    both_left = shift_cols(jnp.concatenate([odd[HALF:], even[HALF:]], axis=0), 1)
    both_right = shift_cols(jnp.concatenate([odd[:HALF], even[:HALF]], axis=0), -1)

    edge, sums, own_mid, before_mid, after_mid = pl.pallas_call(
        products_kernel,
        out_shape=(
            jax.ShapeDtypeStruct((4, DEPTH, DEPTH), BF16),
            jax.ShapeDtypeStruct((2, 2, DEPTH, 2 * PAIR), F32),
            jax.ShapeDtypeStruct((B, 2 * PAIR), F32),
            jax.ShapeDtypeStruct((B, 2 * PAIR), BF16),
            jax.ShapeDtypeStruct((B, 2 * PAIR), BF16),
        ),
        in_specs=[pl.BlockSpec(memory_space=pltpu.SMEM)] + whole(7),
        out_specs=tuple(whole(5)),
        scratch_shapes=[pltpu.VMEM((3, DEPTH, DEPTH), BF16)],
        compiler_params=pltpu.CompilerParams(vmem_limit_bytes=20 << 20),
        cost_estimate=pl.CostEstimate(flops=2 << 30, bytes_accessed=8 << 20, transcendentals=0),
        name="products",
    )(index, slots, restrict, left, own, right, odd, even)
    owned, before, after = pl.pallas_call(
        outer_kernel,
        out_shape=(
            jax.ShapeDtypeStruct((B, 6 * PAIR), F32),
            jax.ShapeDtypeStruct((B, 6 * PAIR), BF16),
            jax.ShapeDtypeStruct((B, 6 * PAIR), BF16),
        ),
        in_specs=whole(8),
        out_specs=tuple(whole(3)),
        compiler_params=pltpu.CompilerParams(vmem_limit_bytes=12 << 20),
        cost_estimate=pl.CostEstimate(flops=1 << 30, bytes_accessed=4 << 20, transcendentals=0),
        name="outer",
    )(edge, sums, restrict, both_left, both_right, own_mid, before_mid, after_mid)
    below = shift_cols(after, 1)
    above = shift_cols(before, -1)
    return pl.pallas_call(
        join_kernel,
        out_shape=jax.ShapeDtypeStruct((1, B, 15 * B), F32),
        in_specs=whole(3),
        out_specs=whole(1)[0],
        compiler_params=pltpu.CompilerParams(vmem_limit_bytes=4 << 20),
        name="join",
    )(owned, below, above)


def solution(mesh):
    return jax.shard_map(
        body,
        mesh=mesh,
        in_specs=(
            P("row", "col", None, None),
            P("row", "col", None),
            P("row", "col"),
            P("row", "col", None, None),
            P("row", "col", None),
            P("row", "col", None, None),
            P("row", "col", None),
        ),
        out_specs=P("row", "col", None),
        check_vma=False,
    )
```

```python
import jax
import jax.numpy as jnp
from jax import lax
from jax.experimental import pallas as pl
from jax.experimental.pallas import tpu as pltpu
from jax.sharding import PartitionSpec as P

PLANE = 256
AGG = 16
HALF = 8
B = 64
KA = 32
PAIR = 2 * B
TILES = KA // 2
EMPTY = 2 * TILES
SPAN = 24
DEPTH = HALF * B

F32 = jnp.float32
BF16 = jnp.bfloat16


def shift_cols(value, step):
    count = lax.axis_size("col")
    return lax.ppermute(value, "col", [(i, (i + step) % count) for i in range(count)])


def swap_rows(value, first):
    pairs = []
    for row in range(first, lax.axis_size("row") - 1, 2):
        pairs += [(row, row + 1), (row + 1, row)]
    return lax.ppermute(value, "row", pairs)


def plane_of(first):
    return 2 * lax.rem(lax.axis_index("row") + first + 1, 2)


def swap_lanes(x):
    return pltpu.roll(x, B, 1)


def flip_mask(cols_ref, q):
    first_own = cols_ref[0:1, q : q + 1] == lax.axis_index("col")
    value = jnp.where(first_own, 1.0, 0.0) if q < HALF else jnp.where(first_own, 0.0, 1.0)
    return jnp.broadcast_to(value, (B, PAIR)) > 0.5


def ordered(x, cols_ref, q):
    return jnp.where(flip_mask(cols_ref, q), swap_lanes(x), x)


def order_kernel(cols_hbm, p_hbm, all_ref, head_ref, tail_ref, cols_ref, raw, sems):
    parts = 2
    size = AGG // parts
    cols_copy = pltpu.make_async_copy(cols_hbm, cols_ref, sems.at[parts])
    cols_copy.start()

    def fetch(part):
        at = pl.ds(part * size, size)
        return pltpu.make_async_copy(p_hbm.at[0, at], raw.at[at], sems.at[part])

    for part in range(parts):
        fetch(part).start()
    cols_copy.wait()
    for part in range(parts):
        fetch(part).wait()
        for q in range(part * size, (part + 1) * size):
            y = ordered(raw[q], cols_ref, q)
            all_ref[q] = y
            if q < HALF:
                head_ref[q] = y
            else:
                tail_ref[q - HALF] = y


def order(p_vals, p_cols):
    half = jax.ShapeDtypeStruct((HALF, B, PAIR), BF16)
    return pl.pallas_call(
        order_kernel,
        out_shape=(jax.ShapeDtypeStruct((AGG, B, PAIR), BF16), half, half),
        in_specs=[pl.BlockSpec(memory_space=pl.ANY)] * 2,
        out_specs=tuple(whole(3)),
        scratch_shapes=[
            pltpu.VMEM((2, AGG), jnp.int32),
            pltpu.VMEM((AGG, B, PAIR), BF16),
            pltpu.SemaphoreType.DMA((3,)),
        ],
        compiler_params=pltpu.CompilerParams(vmem_limit_bytes=4 << 20),
        name="order",
    )(in_hbm(p_cols[0].T), in_hbm(p_vals))


def slot_table(cols, count_ref, wide_ref, table_ref):
    row = lax.broadcasted_iota(jnp.int32, (AGG, KA), 0)
    reach = ((cols & (PLANE - 1)) - lax.axis_index("col") * AGG + HALF) & (PLANE - 1)
    wide_ref[:AGG, :KA] = (cols // PLANE) * SPAN + reach - jnp.where(row < HALF, 0, HALF)
    places = wide_ref[...].T
    slot = lax.broadcasted_iota(jnp.int32, (KA, PAIR), 0)
    dest = lax.broadcasted_iota(jnp.int32, (KA, PAIR), 1)
    entry = slot // 2 + TILES * ((slot + dest) & 1) - EMPTY
    for q in range(AGG):
        place = jnp.broadcast_to(places[:KA, q : q + 1], (KA, PAIR))
        count = jnp.broadcast_to(count_ref[0:1, q : q + 1], (KA, PAIR))
        found = jnp.where((place == dest) & (slot < count), entry, 0)
        table_ref[q : q + 1, :] = EMPTY + jnp.sum(found, axis=0, keepdims=True)


def prepare_kernel(
    links_hbm, count_hbm, cols_hbm, a_hbm, r_hbm, index_ref, slots_ref, restrict_ref,
    links_ref, count_ref, cols_ref, wide_ref, table_ref, raw, sems, small_sems
):
    def fetch(q):
        return pltpu.make_async_copy(a_hbm.at[0, q], slots_ref.at[q, :, pl.ds(0, KA * B)], sems.at[q])

    small = [
        pltpu.make_async_copy(cols_hbm, cols_ref, small_sems.at[0]),
        pltpu.make_async_copy(r_hbm.at[0], raw, small_sems.at[1]),
        pltpu.make_async_copy(links_hbm.at[0], links_ref, small_sems.at[2]),
        pltpu.make_async_copy(count_hbm, count_ref, small_sems.at[3]),
    ]
    for q in range(AGG):
        fetch(q).start()
    for copy in small:
        copy.start(priority=1)

    def row(q, carry):
        slots_ref[q, :, EMPTY * PAIR :] = jnp.zeros((B, PAIR), BF16)
        fetch(q).wait()
        for k in range(TILES):
            x = slots_ref[q, :, k * PAIR : (k + 1) * PAIR]
            slots_ref[q, :, (TILES + k) * PAIR : (TILES + k + 1) * PAIR] = swap_lanes(x)
        return carry

    lax.fori_loop(0, 12, row, 0)
    for copy in small:
        copy.wait()
    slot_table(links_ref[...], count_ref, wide_ref, table_ref)
    to_scalars = pltpu.make_async_copy(table_ref, index_ref, small_sems.at[4])
    to_scalars.start()
    unit = jnp.where(
        lax.broadcasted_iota(jnp.int32, (PAIR, PAIR), 0) == lax.broadcasted_iota(jnp.int32, (PAIR, PAIR), 1), 1.0, 0.0
    ).astype(BF16)
    for q in range(0, AGG, 2):
        two = jnp.concatenate([ordered(raw[q], cols_ref, q), ordered(raw[q + 1], cols_ref, q + 1)], axis=0)
        at = (q % HALF) * B
        turned = lax.dot_general(unit, two, (((1,), (1,)), ((), ())), preferred_element_type=F32)
        restrict_ref[q // HALF, :, at : at + PAIR] = turned.astype(BF16)
    lax.fori_loop(12, AGG, row, 0)
    to_scalars.wait()


def prepare(a_cols, a_count, r_cols, a_vals, r_vals):
    return pl.pallas_call(
        prepare_kernel,
        out_shape=(
            pltpu.SMEM((AGG, PAIR), jnp.int32),
            pltpu.VMEM((AGG, B, (EMPTY + 1) * PAIR), BF16),
            jax.ShapeDtypeStruct((2, PAIR, DEPTH), BF16),
        ),
        in_specs=[pl.BlockSpec(memory_space=pl.ANY)] * 5,
        out_specs=(pl.BlockSpec(memory_space=pltpu.SMEM), *whole(2)),
        scratch_shapes=[
            pltpu.VMEM((AGG, KA), jnp.int32),
            pltpu.VMEM((1, AGG), jnp.int32),
            pltpu.VMEM((2, AGG), jnp.int32),
            pltpu.VMEM((PAIR, PAIR), jnp.int32),
            pltpu.VMEM((AGG, PAIR), jnp.int32),
            pltpu.VMEM((AGG, B, PAIR), BF16),
            pltpu.SemaphoreType.DMA((AGG,)),
            pltpu.SemaphoreType.DMA((5,)),
        ],
        compiler_params=pltpu.CompilerParams(vmem_limit_bytes=12 << 20),
        cost_estimate=pl.CostEstimate(flops=0, bytes_accessed=6 << 20, transcendentals=0),
        name="prepare",
    )(in_hbm(a_cols), in_hbm(a_count), in_hbm(r_cols[0].T), in_hbm(a_vals), in_hbm(r_vals))


def placed(x, shifted):
    if not shifted:
        return x
    lower = lax.broadcasted_iota(jnp.int32, (B, PAIR), 1) < B
    first, second = swap_lanes(x[:, :PAIR]), swap_lanes(x[:, PAIR:])
    return jnp.concatenate([jnp.where(lower, 0.0, first), jnp.where(lower, first, second)], axis=1)


def banded(blocks_ref, against, j):
    mid = DEPTH // 2

    def part(rows, depth):
        return jnp.dot(blocks_ref[rows, depth], against[depth], preferred_element_type=F32)

    everything, first, second = slice(0, DEPTH), slice(0, mid), slice(mid, DEPTH)
    if j == 1:
        return part(everything, everything)
    if j == 0:
        return jnp.concatenate([part(first, everything), part(second, second)], axis=0)
    return jnp.concatenate([part(first, first), part(second, everything)], axis=0)


def merged(low, high):
    lower = lax.broadcasted_iota(jnp.int32, (DEPTH, PAIR), 1) < B
    high = swap_lanes(high)
    return low + jnp.where(lower, 0.0, high), jnp.where(lower, high, 0.0)


def rows_of(ref, start):
    return ref[start : start + HALF].reshape(DEPTH, PAIR)


def gather(index_ref, slots_ref, s, half, j, into):
    lower = lax.broadcasted_iota(jnp.int32, (B, PAIR), 1) < B
    for e in range(HALF):
        q = half * HALF + e
        at = s * SPAN + j * HALF
        for tile in range(HALF // 2):
            rows, cols = slice(e * B, (e + 1) * B), slice(tile * PAIR, (tile + 1) * PAIR)
            if (j == 0 and tile < e // 2) or (j == 2 and tile > e // 2):
                early, near = e < HALF // 2, tile < HALF // 4
                if (j == 0 and (early or not near)) or (j == 2 and (near or not early)):
                    into[rows, cols] = jnp.zeros((B, PAIR), BF16)
                continue
            first = pl.multiple_of(index_ref[q, at + 2 * tile] * PAIR, PAIR)
            second = pl.multiple_of(index_ref[q, at + 2 * tile + 1] * PAIR, PAIR)
            into[rows, cols] = jnp.where(
                lower, slots_ref[q, :, pl.ds(first, PAIR)], slots_ref[q, :, pl.ds(second, PAIR)]
            )


def products_kernel(
    index_ref, slots_ref, restrict_ref, left_ref, own_ref, right_ref, odd_ref, even_ref,
    edge_ref, sums_ref, own_out, before_out, after_out, band
):
    turn = 0
    terms = []
    for n, near in ((2, own_ref), (0, odd_ref), (1, even_ref)):
        s = 1 if n == 2 else plane_of(1 - n)
        for half in range(2):
            sums = [None, None]
            for j in range(3):
                part = half + j
                if part in (0, 3) and n < 2:
                    gather(index_ref, slots_ref, s, half, j, edge_ref.at[2 * n + half])
                    continue
                if part in (0, 3):
                    against = rows_of(right_ref if part else left_ref, 0)
                else:
                    against = rows_of(near, (part - 1) * HALF)
                turn = (turn + 1) % 3
                gather(index_ref, slots_ref, s, half, j, band.at[turn])
                term = banded(band.at[turn], against, j)
                sums[part // 2] = term if sums[part // 2] is None else sums[part // 2] + term
            first, second = merged(*sums)
            if n < 2:
                sums_ref[n, half, :, :PAIR] = first
                sums_ref[n, half, :, PAIR:] = second
            else:
                fine = jnp.concatenate([first.astype(BF16), second.astype(BF16)], axis=1)
                terms.append(jnp.dot(restrict_ref[half], fine, preferred_element_type=F32))
    own_out[...] = terms[0][B:] + terms[1][:B]
    before_out[...] = placed(terms[0][:B], True).astype(BF16)
    after_out[...] = placed(terms[1][B:], True).astype(BF16)


def outer_kernel(
    edge_ref, sums_ref, restrict_ref, left_ref, right_ref, own_mid, before_mid, after_mid,
    own_ref, before_ref, after_ref
):
    lower = lax.broadcasted_iota(jnp.int32, (DEPTH, PAIR), 1) < B
    mid = slice(2 * PAIR, 4 * PAIR)
    own_ref[:, mid] = own_mid[...]
    before_ref[:, mid] = before_mid[...]
    after_ref[:, mid] = after_mid[...]
    for n in range(2):
        terms = []
        for half in range(2):
            first, second = sums_ref[n, half, :, :PAIR], sums_ref[n, half, :, PAIR:]
            against = rows_of(right_ref if half else left_ref, n * HALF)
            if half:
                against = swap_lanes(against)
            term = banded(edge_ref.at[2 * n + half], against, 2 * half)
            if half:
                first = first + jnp.where(lower, 0.0, term)
                second = second + jnp.where(lower, term, 0.0)
            else:
                first = first + term
            fine = jnp.concatenate([first.astype(BF16), second.astype(BF16)], axis=1)
            terms.append(jnp.dot(restrict_ref[half], fine, preferred_element_type=F32))
        cols = pl.ds(pl.multiple_of(plane_of(1 - n) * 2 * PAIR, PAIR), 2 * PAIR)
        own_ref[:, cols] = placed(terms[0][B:] + terms[1][:B], True)
        before_ref[:, cols] = terms[0][:B].astype(BF16)
        after_ref[:, cols] = terms[1][B:].astype(BF16)


OWN_AT = (0, 1, 3, 4, 5, 6)
ABOVE_AT = (1, 2, 3, 4, 6, 7)
BELOW_AT = (0, 1, 2, 3, 5, 6)


def join_kernel(own_ref, below_ref, above_ref, out_ref):
    for tile in range(8):
        width = PAIR if tile < 7 else B
        total = None
        for ref, places in ((own_ref, OWN_AT), (above_ref, ABOVE_AT), (below_ref, BELOW_AT)):
            if tile in places:
                at = places.index(tile) * PAIR
                piece = ref[:, at : at + width].astype(F32)
                total = piece if total is None else total + piece
        out_ref[0, :, tile * PAIR : tile * PAIR + width] = total


def in_hbm(x):
    return pltpu.with_memory_space_constraint(x, pltpu.HBM)


def whole(count):
    return [pl.BlockSpec(memory_space=pltpu.VMEM)] * count


def body(a_vals, a_cols, a_count, p_vals, p_cols, r_vals, r_cols):
    own, head, tail = order(p_vals, p_cols)
    odd = swap_rows(own, 1)
    even = swap_rows(own, 0)
    left = shift_cols(tail, 1)
    right = shift_cols(head, -1)
    index, slots, restrict = prepare(a_cols, a_count, r_cols, a_vals, r_vals)
    even, odd, left, right, slots = lax.optimization_barrier((even, odd, left, right, slots))
    both_left = shift_cols(jnp.concatenate([odd[HALF:], even[HALF:]], axis=0), 1)
    both_right = shift_cols(jnp.concatenate([odd[:HALF], even[:HALF]], axis=0), -1)

    edge, sums, own_mid, before_mid, after_mid = pl.pallas_call(
        products_kernel,
        out_shape=(
            jax.ShapeDtypeStruct((4, DEPTH, DEPTH), BF16),
            jax.ShapeDtypeStruct((2, 2, DEPTH, 2 * PAIR), F32),
            jax.ShapeDtypeStruct((B, 2 * PAIR), F32),
            jax.ShapeDtypeStruct((B, 2 * PAIR), BF16),
            jax.ShapeDtypeStruct((B, 2 * PAIR), BF16),
        ),
        in_specs=[pl.BlockSpec(memory_space=pltpu.SMEM)] + whole(7),
        out_specs=tuple(whole(5)),
        scratch_shapes=[pltpu.VMEM((3, DEPTH, DEPTH), BF16)],
        compiler_params=pltpu.CompilerParams(vmem_limit_bytes=20 << 20),
        cost_estimate=pl.CostEstimate(flops=2 << 30, bytes_accessed=8 << 20, transcendentals=0),
        name="products",
    )(index, slots, restrict, left, own, right, odd, even)
    owned, before, after = pl.pallas_call(
        outer_kernel,
        out_shape=(
            jax.ShapeDtypeStruct((B, 6 * PAIR), F32),
            jax.ShapeDtypeStruct((B, 6 * PAIR), BF16),
            jax.ShapeDtypeStruct((B, 6 * PAIR), BF16),
        ),
        in_specs=whole(8),
        out_specs=tuple(whole(3)),
        compiler_params=pltpu.CompilerParams(vmem_limit_bytes=12 << 20),
        cost_estimate=pl.CostEstimate(flops=1 << 30, bytes_accessed=4 << 20, transcendentals=0),
        name="outer",
    )(edge, sums, restrict, both_left, both_right, own_mid, before_mid, after_mid)
    below = shift_cols(after, 1)
    above = shift_cols(before, -1)
    return pl.pallas_call(
        join_kernel,
        out_shape=jax.ShapeDtypeStruct((1, B, 15 * B), F32),
        in_specs=whole(3),
        out_specs=whole(1)[0],
        compiler_params=pltpu.CompilerParams(vmem_limit_bytes=4 << 20),
        name="join",
    )(owned, below, above)


def solution(mesh):
    return jax.shard_map(
        body,
        mesh=mesh,
        in_specs=(
            P("row", "col", None, None),
            P("row", "col", None),
            P("row", "col"),
            P("row", "col", None, None),
            P("row", "col", None),
            P("row", "col", None, None),
            P("row", "col", None),
        ),
        out_specs=P("row", "col", None),
        check_vma=False,
    )
```
